32 devices in a mesh: tm: 8 (over y, x, core), row: 4 (over z).
Axes of the slice: x: 2, y: 2, z: 4, core: 2. Of those that a mesh axis runs over, the one named last changes fastest.
Arguments:
- frames_in: bfloat16 [32, 16, 64, 512], P('tm', 'row'), may hold values from -6 to 6
- state_in: float32 [16, 64, 512], P('row'), may hold values from -12 to 12
- modulus: float32 [32, 256], replicated, may hold values from 0.05 to 1
- angle: float32 [256], replicated, may hold values from -3.140625 to 3.140625
- w_in: bfloat16 [3, 3, 512, 512], replicated, may hold values from -0.09375 to 0.09375
- w_out: bfloat16 [3, 3, 512, 512], replicated, may hold values from -0.0234375 to 0.0234375
Outputs:
- output: bfloat16 [32, 16, 64, 512], P('tm', 'row')
The draws below stay inside these ranges and needn't reach their ends.
All inputs are finite; a program needn't handle non-finite values.
Results may differ from the reference program's by a relative error of at most 0.005.
Values may be sent and summed in bfloat16 or wider, within the bound.
A program may use at most 64 MiB of HBM per device.

```python
import jax
import jax.numpy as jnp
from jax import lax

C = 512
PAIRS = 256
W = 64
H = 16
SPAN_SNAPSHOTS = 32


def draw_modulus(key, part):
    gradual_seed, root_seed, quick_seed, multiplier_seed, spike_seed, layers_seed = jax.random.split(jax.random.fold_in(key, 7), 6)
    share = 0.5
    slow_pick = jax.random.uniform(gradual_seed, (PAIRS,), jnp.float32) < share
    slow_gap = jnp.exp(jax.random.uniform(root_seed, (PAIRS,), jnp.float32, jnp.log(0.001), jnp.log(0.01)))
    fast_rate = jax.random.uniform(quick_seed, (PAIRS,), jnp.float32, 0.6, 0.9)
    base_rate = jnp.where(slow_pick, 1.0 - slow_gap, fast_rate)
    factor = jnp.exp(jax.random.uniform(multiplier_seed, (SPAN_SNAPSHOTS, PAIRS), jnp.float32, -jnp.log(2.0), jnp.log(2.0)))
    damping_speeds = jnp.exp(jnp.log(base_rate)[None, :] * factor)
    spike_place = jax.random.randint(spike_seed, (3,), 0, SPAN_SNAPSHOTS)
    hidden_dimension = jax.random.uniform(layers_seed, (3, PAIRS), jnp.float32, 0.5, 0.8)
    snapshot_times = jnp.arange(SPAN_SNAPSHOTS)
    for spike_ordinal in range(3):
        spike_markers = (snapshot_times == spike_place[spike_ordinal])[:, None]
        damping_speeds = jnp.where(spike_markers, damping_speeds * hidden_dimension[spike_ordinal][None, :], damping_speeds)
    return damping_speeds.astype(jnp.float32)


def block_scale(key, extent, pieces, smallest, top_value):
    factor_of = 1.0
    for position, shards_of in pieces:
        steps = jax.random.uniform(jax.random.fold_in(jax.random.fold_in(key, 6), position), (shards_of,), jnp.float32, smallest / len(pieces), top_value / len(pieces))
        factor_of = factor_of * jnp.repeat(jnp.exp(steps), extent[position] // shards_of).reshape((-1,) + (1,) * (len(extent) - 1 - position))
    return factor_of


def noise(rng, extent, deviation, bound, shards=(), dtype=jnp.bfloat16):
    values = jax.random.normal(rng, extent, jnp.float32) * deviation
    if len(shards) > 0:
        values = block_scale(rng, extent, shards, -0.22, 0.18) * values
    return jnp.clip(values, min=-bound, max=bound).astype(dtype)


def setup_inputs(seed: int = 0) -> dict:
    key_list = jax.random.split(jax.random.key(seed), 7)
    frames_in = noise(key_list[0], (SPAN_SNAPSHOTS, H, W, C), 1.0, 6.0, ((0, 8), (1, 4)))
    state_in = noise(key_list[1], (H, W, C), 2.0, 12.0, ((0, 4),), jnp.float32)
    modulus = draw_modulus(jax.random.fold_in(key_list[6], 71), 0)
    angle = jnp.clip(jax.random.uniform(key_list[3], (PAIRS,), jnp.float32, -3.140625, 3.140625), -3.140625, 3.140625)
    w_in = noise(key_list[4], (3, 3, C, C), (9 * C) ** -0.5, 0.09375)
    w_out = noise(key_list[5], (3, 3, C, C), (144 * C) ** -0.5, 0.0234375)
    return {"frames_in": frames_in, "state_in": state_in, "modulus": modulus, "angle": angle, "w_in": w_in, "w_out": w_out}


def conv_frame(source, weight):
    padded = jnp.pad(source, ((1, 1), (1, 1), (0, 0)))
    height, columns, channels = source.shape
    summed = jnp.zeros((height * columns, weight.shape[3]), jnp.float32)
    for row_tap in range(3):
        for col_tap in range(3):
            window = padded[row_tap:row_tap + height, col_tap:col_tap + columns, :].reshape(-1, channels)
            summed = summed + jnp.dot(window, weight[row_tap, col_tap], preferred_element_type=jnp.float32)
    return summed.reshape(height, columns, -1)


def rotate(rate_re, rate_im, values):
    half = values.shape[-1] // 2
    part_re = values[..., :half]
    part_im = values[..., half:]
    return jnp.concatenate([rate_re * part_re - rate_im * part_im, rate_im * part_re + rate_re * part_im], axis=-1)


def reference(frames_in, state_in, modulus, angle, w_in, w_out):
    rate_re = modulus * jnp.cos(angle)[None, :]
    rate_im = modulus * jnp.sin(angle)[None, :]

    def advance(carried, inputs):
        one_frame, step_re, step_im = inputs
        update = conv_frame(one_frame, w_in)
        carried = rotate(step_re, step_im, carried) + update
        state_bf = carried.astype(jnp.bfloat16)
        result = jax.nn.gelu(conv_frame(state_bf, w_out), approximate=False).astype(jnp.bfloat16)
        return carried, result

    _, output = lax.scan(advance, state_in.astype(jnp.float32), (frames_in, rate_re, rate_im))
    return output
```

```python
import functools

import jax
import jax.numpy as jnp
from jax import lax
from jax.experimental import pallas as pl
from jax.experimental.pallas import tpu as pltpu
from jax.sharding import PartitionSpec as P

MESH = pl.DeviceIdType.MESH
F32 = jnp.float32
BF16 = jnp.bfloat16


def gelu(v):
    return v * (0.5 + 0.5 * lax.erf(v * 0.7071067811865476))


def rot(re, im, v):
    half = v.shape[-1] // 2
    p, q = v[:, :half], v[:, half:]
    return jnp.concatenate([re * p - im * q, im * p + re * q], axis=-1)


def kernel(
    n_tm, n_row, steps,
    frames_hbm, state_hbm, mod_ref, ang_ref, win_hbm, wout_hbm, out_ref,
    frames_v, state_v, win, wout, x1, x2, acc, loc, tab_re, tab_im,
    t_buf, r_buf, s_send, s_recv, fh_recv, lh_send, lh_recv, ih_send, ih_recv,
    load_sem, s_ssem, s_rsem, fh_ssem, fh_rsem, lh_ssem, lh_rsem, ih_ssem, ih_rsem,
):
    F, R, W, C = frames_hbm.shape
    half = C // 2
    FW = F * W
    K3 = 3 * C
    me = lax.axis_index("tm")
    row = lax.axis_index("row")
    has_up, has_down = row > 0, row < n_row - 1
    sides = ((has_up, row - 1), (has_down, row + 1))
    partners = [me + (1 - 2 * ((me >> k) & 1)) * (1 << k) for k in range(steps)]

    ld_frames = pltpu.make_async_copy(frames_hbm, frames_v, load_sem.at[0])
    ld_frames.start()
    ld_win = pltpu.make_async_copy(win_hbm, win, load_sem.at[1])
    ld_win.start()
    ld_state = pltpu.make_async_copy(state_hbm, state_v, load_sem.at[2])
    ld_state.start()
    ld_wout = pltpu.make_async_copy(wout_hbm, wout, load_sem.at[3])

    barrier = pltpu.get_barrier_semaphore()
    for p in partners:
        pl.semaphore_signal(barrier, inc=1, device_id={"tm": p}, device_id_type=MESH)
    for has, where in sides:
        @pl.when(has)
        def _():
            pl.semaphore_signal(barrier, inc=1, device_id={"row": where}, device_id_type=MESH)
    pl.semaphore_wait(barrier, steps + has_up.astype(jnp.int32) + has_down.astype(jnp.int32))

    def remote(src, dst, ssem, rsem, dev):
        return pltpu.make_async_remote_copy(
            src_ref=src, dst_ref=dst, send_sem=ssem, recv_sem=rsem,
            device_id=dev, device_id_type=MESH,
        )

    edge = (0, R - 1)
    fh = [
        remote(frames_hbm.at[:, edge[s]], fh_recv.at[1 - s], fh_ssem.at[s], fh_rsem.at[1 - s],
               {"row": sides[s][1]})
        for s in range(2)
    ]
    fh_in = [
        remote(frames_hbm.at[:, edge[s]], fh_recv.at[s], fh_ssem.at[s], fh_rsem.at[s],
               {"row": sides[s][1]})
        for s in range(2)
    ]
    for s in range(2):
        @pl.when(sides[s][0])
        def _():
            fh[s].start()

    rows = tab_re.shape[0]
    idx = lax.broadcasted_iota(jnp.int32, (rows, 1), 0)
    lo = jnp.zeros((rows, 1), jnp.int32)
    hi = jnp.zeros((rows, 1), jnp.int32)
    keep = jnp.ones((rows, 1), jnp.int32)
    for t in range(F):
        lo = jnp.where(idx == t, me * F + t, lo)
        hi = jnp.where(idx == t, me * F + t + 1, hi)
        lo = jnp.where(idx == F + t, me * F, lo)
        hi = jnp.where(idx == F + t, me * F + t + 1, hi)
    ups = []
    for k in range(steps):
        size = 1 << k
        up = (me >> k) & 1
        ups.append(up)
        base = (me >> k) << k
        top = ((me >> k) | 1) << k
        i_a, i_b = 2 * F + k, 2 * F + steps + k
        lo = jnp.where(idx == i_a, top * F, lo)
        hi = jnp.where(idx == i_a, (top + size) * F, hi)
        lo = jnp.where(idx == i_b, base * F, lo)
        hi = jnp.where(idx == i_b, me * F, hi)
        keep = jnp.where(idx == i_b, up, keep)
    mod = jnp.ones((rows, half), F32) * keep.astype(F32)
    for f in range(n_tm * F):
        mod = mod * jnp.where((lo <= f) & (f < hi), mod_ref[f:f + 1, :], 1.0)
    phase = (hi - lo).astype(F32) * ang_ref[...]
    tab_re[...] = mod * jnp.cos(phase)
    tab_im[...] = mod * jnp.sin(phase)

    def table(i):
        return tab_re[i:i + 1, :], tab_im[i:i + 1, :]

    def spread(x, r, f0, v):
        n = v.shape[0]
        col = lax.broadcasted_iota(jnp.int32, (n, 1), 0) % W
        at = slice(f0 * W, f0 * W + n)
        x[r, at, C:2 * C] = v.astype(BF16)
        x[r, at, 0:C] = jnp.where(col == 0, 0.0, pltpu.roll(v, 1, 0)).astype(BF16)
        x[r, at, 2 * C:] = jnp.where(col == W - 1, 0.0, pltpu.roll(v, n - 1, 0)).astype(BF16)

    def taps(x, w, r0, count, a0, a1):
        m = count * FW
        lhs = jnp.concatenate(
            [x[r0 + a:r0 + a + count].reshape(m, K3) for a in range(a0, a1)], axis=-1
        )
        return jnp.dot(lhs, w[a0 * K3:a1 * K3, :], preferred_element_type=F32).reshape(count, FW, C)

    order = list(range(1, R - 1)) + [0, R - 1]
    groups = ((0, R - 2), (R - 2, R))
    first = (me == 0).astype(F32)

    def local_scan(g):
        for pos in range(*groups[g]):
            r = order[pos]
            run = state_v[r] * first
            for t in range(F):
                run = rot(*table(t), run) + acc[r, t * W:(t + 1) * W]
                loc[r, t * W:(t + 1) * W] = run
            t_buf[pos] = run
            s_send[0, pos] = run.astype(BF16)
            r_buf[pos] = jnp.zeros_like(run)

    def hop(k, g):
        at = pl.ds(groups[g][0], groups[g][1] - groups[g][0])
        return remote(s_send.at[k, at], s_recv.at[k, at], s_ssem.at[k, g], s_rsem.at[k, g],
                      {"tm": partners[k]})

    def combine(k, g):
        hop(k, g).wait_recv()
        up = ups[k] == 1
        for pos in range(*groups[g]):
            got = s_recv[k, pos].astype(F32)
            if k < steps - 1:
                mine = t_buf[pos]
                low = jnp.where(up, got, mine)
                high = jnp.where(up, mine, got)
                new = rot(*table(2 * F + k), low) + high
                t_buf[pos] = new
                s_send[k + 1, pos] = new.astype(BF16)
            r_buf[pos] = r_buf[pos] + rot(*table(2 * F + steps + k), got)
        if k < steps - 1:
            hop(k + 1, g).start()

    def states(g):
        for pos in range(*groups[g]):
            r = order[pos]
            for t in range(F):
                v = loc[r, t * W:(t + 1) * W] + rot(*table(F + t), r_buf[pos])
                spread(x2, r + 1, t, v)

    ld_frames.wait()
    for r in range(R):
        spread(x1, r + 1, 0, frames_v[:, r].reshape(FW, C).astype(F32))
    ld_win.wait()
    ld_wout.start()
    acc[1:R - 1] = taps(x1, win, 1, R - 2, 0, 3)
    ld_state.wait()
    local_scan(0)
    hop(0, 0).start()
    acc[0:1] = taps(x1, win, 0, 1, 1, 3)
    combine(0, 0)
    acc[R - 1:R] = taps(x1, win, R - 1, 1, 0, 2)
    if steps > 1:
        combine(1, 0)
    for s in range(2):
        @pl.when(sides[s][0])
        def _():
            fh_in[s].wait_recv()
            spread(x1, s * (R + 1), 0, fh_recv[s].reshape(FW, C).astype(F32))

        @pl.when(jnp.logical_not(sides[s][0]))
        def _():
            x1[s * (R + 1)] = jnp.zeros((FW, K3), BF16)
    acc[0:1] += taps(x1, win, 0, 1, 0, 1)
    acc[R - 1:R] += taps(x1, win, R - 1, 1, 2, 3)
    local_scan(1)
    hop(0, 1).start()

    lh = [
        remote(lh_send.at[s], lh_recv.at[1 - s], lh_ssem.at[s], lh_rsem.at[1 - s],
               {"row": sides[s][1]})
        for s in range(2)
    ]
    lh_in = [
        remote(lh_send.at[s], lh_recv.at[s], lh_ssem.at[s], lh_rsem.at[s], {"row": sides[s][1]})
        for s in range(2)
    ]
    ih = [
        remote(ih_send.at[s], ih_recv.at[1 - s], ih_ssem.at[s], ih_rsem.at[1 - s],
               {"row": sides[s][1]})
        for s in range(2)
    ]
    ih_in = [
        remote(ih_send.at[s], ih_recv.at[s], ih_ssem.at[s], ih_rsem.at[s], {"row": sides[s][1]})
        for s in range(2)
    ]
    for s in range(2):
        lh_send[s] = loc[edge[s]].astype(BF16)

        @pl.when(sides[s][0])
        def _():
            lh[s].start()

    for k in range(2, steps):
        combine(k, 0)
    ld_wout.wait()
    states(0)
    acc[1:2] = taps(x2, wout, 1, 1, 1, 3)
    combine(0, 1)
    acc[R - 2:R - 1] = taps(x2, wout, R - 2, 1, 0, 2)
    if steps > 1:
        combine(1, 1)
    acc[0:1] = taps(x2, wout, 0, 1, 2, 3)
    acc[R - 1:R] = taps(x2, wout, R - 1, 1, 0, 1)
    for k in range(2, steps):
        combine(k, 1)
    for s in range(2):
        ih_send[s] = r_buf[R - 2 + s].astype(BF16)

        @pl.when(sides[s][0])
        def _():
            ih[s].start()
    states(1)

    def finish(r, v):
        out_ref[:, r] = gelu(v).astype(BF16).reshape(F, W, C)

    acc[0:1] += taps(x2, wout, 0, 1, 1, 2)
    acc[R - 1:R] += taps(x2, wout, R - 1, 1, 1, 2)
    finish(1, acc[1] + taps(x2, wout, 1, 1, 0, 1)[0])
    finish(R - 2, acc[R - 2] + taps(x2, wout, R - 2, 1, 2, 3)[0])
    for s in range(2):
        @pl.when(sides[s][0])
        def _():
            lh_in[s].wait_recv()
            ih_in[s].wait_recv()
            inc = ih_recv[s].astype(F32)
            for t in range(F):
                spread(x2, s * (R + 1), t, lh_recv[s, t * W:(t + 1) * W].astype(F32)
                       + rot(*table(F + t), inc))

        @pl.when(jnp.logical_not(sides[s][0]))
        def _():
            x2[s * (R + 1)] = jnp.zeros((FW, K3), BF16)
    finish(0, acc[0] + taps(x2, wout, 0, 1, 0, 1)[0])
    finish(R - 1, acc[R - 1] + taps(x2, wout, R - 1, 1, 2, 3)[0])

    for k in range(steps):
        for g in range(2):
            hop(k, g).wait_send()
    for s in range(2):
        @pl.when(sides[s][0])
        def _():
            fh[s].wait_send()
            lh[s].wait_send()
            ih[s].wait_send()


def solution(mesh):
    n_tm, n_row = mesh.shape["tm"], mesh.shape["row"]
    steps = n_tm.bit_length() - 1
    assert n_tm == 1 << steps

    def shards(frames_in, state_in, modulus, angle, w_in, w_out):
        F, R, W, C = frames_in.shape
        assert R >= 4
        n_table = -(-(2 * F + 2 * steps) // 8) * 8
        anywhere = pl.BlockSpec(memory_space=pl.ANY)
        vmem = pl.BlockSpec(memory_space=pltpu.VMEM)
        dma = pltpu.SemaphoreType.DMA
        FW = F * W
        return pl.pallas_call(
            functools.partial(kernel, n_tm, n_row, steps),
            out_shape=jax.ShapeDtypeStruct(frames_in.shape, BF16),
            in_specs=[anywhere, anywhere, vmem, vmem, anywhere, anywhere],
            out_specs=vmem,
            scratch_shapes=[
                pltpu.VMEM((F, R, W, C), BF16),
                pltpu.VMEM((R, W, C), F32),
                pltpu.VMEM((9 * C, C), BF16),
                pltpu.VMEM((9 * C, C), BF16),
                pltpu.VMEM((R + 2, FW, 3 * C), BF16),
                pltpu.VMEM((R + 2, FW, 3 * C), BF16),
                pltpu.VMEM((R, FW, C), F32),
                pltpu.VMEM((R, FW, C), F32),
                pltpu.VMEM((n_table, C // 2), F32),
                pltpu.VMEM((n_table, C // 2), F32),
                pltpu.VMEM((R, W, C), F32),
                pltpu.VMEM((R, W, C), F32),
                pltpu.VMEM((steps, R, W, C), BF16),
                pltpu.VMEM((steps, R, W, C), BF16),
                pltpu.VMEM((2, F, W, C), BF16),
                pltpu.VMEM((2, FW, C), BF16),
                pltpu.VMEM((2, FW, C), BF16),
                pltpu.VMEM((2, W, C), BF16),
                pltpu.VMEM((2, W, C), BF16),
                dma((4,)),
                dma((steps, 2)),
                dma((steps, 2)),
                dma((2,)),
                dma((2,)),
                dma((2,)),
                dma((2,)),
                dma((2,)),
                dma((2,)),
            ],
            compiler_params=pltpu.CompilerParams(
                collective_id=0, has_side_effects=True, vmem_limit_bytes=56 * 1024 * 1024
            ),
        )(
            frames_in, state_in, modulus, angle.reshape(1, -1),
            w_in.reshape(9 * C, C), w_out.reshape(9 * C, C),
        )

    return jax.shard_map(
        shards,
        mesh=mesh,
        in_specs=(P("tm", "row", None, None), P("row", None, None), P(), P(), P(), P()),
        out_specs=P("tm", "row", None, None),
        check_vma=False,
    )
```

```python
import functools

import jax
import jax.numpy as jnp
from jax import lax
from jax.experimental import pallas as pl
from jax.experimental.pallas import tpu as pltpu
from jax.sharding import PartitionSpec as P

MESH = pl.DeviceIdType.MESH
F32 = jnp.float32
BF16 = jnp.bfloat16


def gelu(v):
    return v * (0.5 + 0.5 * lax.erf(v * 0.7071067811865476))


def rot(re, im, v):
    half = v.shape[-1] // 2
    p, q = v[:, :half], v[:, half:]
    return jnp.concatenate([re * p - im * q, im * p + re * q], axis=-1)


def kernel(
    n_tm, n_row, steps,
    frames_hbm, state_hbm, mod_ref, ang_ref, win_hbm, wout_hbm, out_ref,
    frames_v, state_v, win, wout, x1, x2, acc, loc, tab_re, tab_im,
    t_buf, r_buf, s_send, s_recv, fh_recv, lh_send, lh_recv, ih_send, ih_recv, c_send, c_recv,
    load_sem, s_ssem, s_rsem, fh_ssem, fh_rsem, lh_ssem, lh_rsem, ih_ssem, ih_rsem, c_ssem, c_rsem,
):
    F, R, W, C = frames_hbm.shape
    half = C // 2
    FW = F * W
    K3 = 3 * C
    me = lax.axis_index("tm")
    row = lax.axis_index("row")
    has_up, has_down = row > 0, row < n_row - 1
    sides = ((has_up, row - 1), (has_down, row + 1))
    core = me & 1
    chip = me - core
    partners = [me + (1 - 2 * ((me >> k) & 1)) * (1 << k) for k in range(steps)]

    ld_frames = pltpu.make_async_copy(frames_hbm, frames_v, load_sem.at[0])
    ld_frames.start()
    ld_win = pltpu.make_async_copy(win_hbm, win, load_sem.at[1])
    ld_win.start()
    ld_state = pltpu.make_async_copy(state_hbm, state_v, load_sem.at[2])
    ld_state.start()
    ld_wout = pltpu.make_async_copy(wout_hbm, wout, load_sem.at[3])

    barrier = pltpu.get_barrier_semaphore()
    for p in partners:
        pl.semaphore_signal(barrier, inc=1, device_id={"tm": p}, device_id_type=MESH)
    for has, where in sides:
        @pl.when(has)
        def _():
            for other in (me, partners[0]):
                pl.semaphore_signal(
                    barrier, inc=1, device_id={"tm": other, "row": where}, device_id_type=MESH
                )
    near = has_up.astype(jnp.int32) + has_down.astype(jnp.int32)
    pl.semaphore_wait(barrier, steps + 2 * near)

    def remote(src, dst, ssem, rsem, dev):
        return pltpu.make_async_remote_copy(
            src_ref=src, dst_ref=dst, send_sem=ssem, recv_sem=rsem,
            device_id=dev, device_id_type=MESH,
        )

    edge = (0, R - 1)
    fh = [
        remote(frames_hbm.at[:, edge[s]], fh_recv.at[1 - s], fh_ssem.at[s], fh_rsem.at[1 - s],
               {"row": sides[s][1]})
        for s in range(2)
    ]
    fh_in = [
        remote(frames_hbm.at[:, edge[s]], fh_recv.at[s], fh_ssem.at[s], fh_rsem.at[s],
               {"row": sides[s][1]})
        for s in range(2)
    ]
    for s in range(2):
        @pl.when(sides[s][0])
        def _():
            fh[s].start()

    rows = tab_re.shape[0]
    idx = lax.broadcasted_iota(jnp.int32, (rows, 1), 0)
    lo = jnp.zeros((rows, 1), jnp.int32)
    hi = jnp.zeros((rows, 1), jnp.int32)
    keep = jnp.ones((rows, 1), jnp.int32)
    for t in range(F):
        lo = jnp.where(idx == t, me * F + t, lo)
        hi = jnp.where(idx == t, me * F + t + 1, hi)
        lo = jnp.where(idx == F + t, me * F, lo)
        hi = jnp.where(idx == F + t, me * F + t + 1, hi)
    ups = []
    for k in range(steps):
        size = 1 << k
        up = (me >> k) & 1
        ups.append(up)
        base = (me >> k) << k if k else chip
        top = ((me >> k) | 1) << k
        i_a, i_b = 2 * F + k, 2 * F + steps + k
        lo = jnp.where(idx == i_a, top * F, lo)
        hi = jnp.where(idx == i_a, (top + size) * F, hi)
        lo = jnp.where(idx == i_b, base * F, lo)
        hi = jnp.where(idx == i_b, chip * F if k else me * F, hi)
        if k:
            keep = jnp.where(idx == i_b, up, keep)
    mod = jnp.ones((rows, half), F32) * keep.astype(F32)
    for f in range(n_tm * F):
        mod = mod * jnp.where((lo <= f) & (f < hi), mod_ref[f:f + 1, :], 1.0)
    phase = (hi - lo).astype(F32) * ang_ref[...]
    tab_re[...] = mod * jnp.cos(phase)
    tab_im[...] = mod * jnp.sin(phase)

    def table(i):
        return tab_re[i:i + 1, :], tab_im[i:i + 1, :]

    def spread(x, r, f0, v):
        n = v.shape[0]
        col = lax.broadcasted_iota(jnp.int32, (n, 1), 0) % W
        at = slice(f0 * W, f0 * W + n)
        x[r, at, C:2 * C] = v.astype(BF16)
        x[r, at, 0:C] = jnp.where(col == 0, 0.0, pltpu.roll(v, 1, 0)).astype(BF16)
        x[r, at, 2 * C:] = jnp.where(col == W - 1, 0.0, pltpu.roll(v, n - 1, 0)).astype(BF16)

    def taps(x, w, r0, count, a0, a1):
        m = count * FW
        lhs = jnp.concatenate(
            [x[r0 + a:r0 + a + count].reshape(m, K3) for a in range(a0, a1)], axis=-1
        )
        return jnp.dot(lhs, w[a0 * K3:a1 * K3, :], preferred_element_type=F32).reshape(count, FW, C)

    order = list(range(1, R - 1)) + [0, R - 1]
    groups = ((0, R - 2), (R - 2, R))
    first = (me == 0).astype(F32)

    def local_scan(g):
        for pos in range(*groups[g]):
            r = order[pos]
            run = state_v[r] * first
            for t in range(F):
                run = rot(*table(t), run) + acc[r, t * W:(t + 1) * W]
                loc[r, t * W:(t + 1) * W] = run
            t_buf[pos] = run
            s_send[0, pos] = run.astype(BF16)
            r_buf[pos] = jnp.zeros_like(run)

    def own(g):
        count = (groups[g][1] - groups[g][0]) // 2
        return groups[g][0] + core * count, count

    def hop(k, g):
        start, count = own(g)
        at = pl.ds(start, count) if k else pl.ds(groups[g][0], 2 * count)
        return remote(s_send.at[k, at], s_recv.at[k, at], s_ssem.at[k, g], s_rsem.at[k, g],
                      {"tm": partners[k]})

    def combine(k, g):
        hop(k, g).wait_recv()
        up = ups[k] == 1
        start, count = own(g)
        for i in range(count):
            pos = start + i
            got = s_recv[k, pos].astype(F32)
            if k < steps - 1:
                mine = t_buf[pos]
                low = jnp.where(up, got, mine)
                high = jnp.where(up, mine, got)
                new = rot(*table(2 * F + k), low) + high
                t_buf[pos] = new
                s_send[k + 1, pos] = new.astype(BF16)
            if k:
                r_buf[pos] = r_buf[pos] + rot(*table(2 * F + steps + k), got)
        if k < steps - 1:
            hop(k + 1, g).start()

    def swap(g, mine):
        start, count = own(g)
        if not mine:
            start = groups[g][0] + (1 - core) * count
        at = pl.ds(start, count)
        return remote(c_send.at[at], c_recv.at[at], c_ssem.at[g], c_rsem.at[g],
                      {"tm": partners[0]})

    def share(g):
        start, count = own(g)
        for i in range(count):
            c_send[start + i] = r_buf[start + i].astype(BF16)
        swap(g, True).start()

    def settle(g):
        swap(g, False).wait_recv()
        start, count = own(g)
        for i in range(count):
            pos = groups[g][0] + (1 - core) * count + i
            r_buf[pos] = c_recv[pos].astype(F32)
        for pos in range(*groups[g]):
            r_buf[pos] = rot(*table(2 * F + steps), r_buf[pos]) + core.astype(F32) * s_recv[
                0, pos
            ].astype(F32)

    def states(g):
        for pos in range(*groups[g]):
            r = order[pos]
            for t in range(F):
                v = loc[r, t * W:(t + 1) * W] + rot(*table(F + t), r_buf[pos])
                spread(x2, r + 1, t, v)

    ld_frames.wait()
    for r in range(R):
        spread(x1, r + 1, 0, frames_v[:, r].reshape(FW, C).astype(F32))
    ld_win.wait()
    ld_wout.start()
    acc[1:R - 1] = taps(x1, win, 1, R - 2, 0, 3)
    ld_state.wait()
    local_scan(0)
    hop(0, 0).start()
    acc[0:1] = taps(x1, win, 0, 1, 1, 3)
    combine(0, 0)
    acc[R - 1:R] = taps(x1, win, R - 1, 1, 0, 2)
    for s in range(2):
        @pl.when(sides[s][0])
        def _():
            fh_in[s].wait_recv()
            spread(x1, s * (R + 1), 0, fh_recv[s].reshape(FW, C).astype(F32))

        @pl.when(jnp.logical_not(sides[s][0]))
        def _():
            x1[s * (R + 1)] = jnp.zeros((FW, K3), BF16)
    acc[0:1] += taps(x1, win, 0, 1, 0, 1)
    acc[R - 1:R] += taps(x1, win, R - 1, 1, 2, 3)
    local_scan(1)
    hop(0, 1).start()
    combine(1, 0)

    lh = [
        remote(lh_send.at[s], lh_recv.at[1 - s], lh_ssem.at[s], lh_rsem.at[1 - s],
               {"row": sides[s][1]})
        for s in range(2)
    ]
    lh_in = [
        remote(lh_send.at[s], lh_recv.at[s], lh_ssem.at[s], lh_rsem.at[s], {"row": sides[s][1]})
        for s in range(2)
    ]
    ih = [
        remote(ih_send.at[j], ih_recv.at[1 - core], ih_ssem.at[j], ih_rsem.at[1 - core],
               {"tm": chip + j, "row": row - 1 + 2 * core})
        for j in range(2)
    ]
    ih_out = jnp.where(core == 0, row > 0, row < n_row - 1)
    ih_in = [
        remote(ih_send.at[s], ih_recv.at[s], ih_ssem.at[s], ih_rsem.at[s], {"row": sides[s][1]})
        for s in range(2)
    ]
    for s in range(2):
        lh_send[s] = loc[edge[s]].astype(BF16)

        @pl.when(sides[s][0])
        def _():
            lh[s].start()

    combine(0, 1)
    for k in range(2, steps):
        combine(k, 0)
    share(0)
    combine(1, 1)
    ld_wout.wait()
    settle(0)
    states(0)
    acc[1:2] = taps(x2, wout, 1, 1, 1, 3)
    for k in range(2, steps):
        combine(k, 1)
    pos = R - 2 + core
    inc = r_buf[pos]
    rate = [jnp.where(core == 0, a, b) for a, b in zip(table(2 * F - 1), table(2 * F + steps))]
    early = jnp.where(core == 0, s_send[0, pos].astype(F32), s_recv[0, pos].astype(F32))
    ih_send[0] = inc.astype(BF16)
    ih_send[1] = (rot(*rate, inc) + early).astype(BF16)

    @pl.when(ih_out)
    def _():
        for j in range(2):
            ih[j].start()

    share(1)
    acc[R - 2:R - 1] = taps(x2, wout, R - 2, 1, 0, 2)
    acc[0:1] = taps(x2, wout, 0, 1, 2, 3)
    acc[R - 1:R] = taps(x2, wout, R - 1, 1, 0, 1)
    settle(1)
    states(1)

    def finish(r, v):
        out_ref[:, r] = gelu(v).astype(BF16).reshape(F, W, C)

    acc[0:1] += taps(x2, wout, 0, 1, 1, 2)
    acc[R - 1:R] += taps(x2, wout, R - 1, 1, 1, 2)
    finish(1, acc[1] + taps(x2, wout, 1, 1, 0, 1)[0])
    finish(R - 2, acc[R - 2] + taps(x2, wout, R - 2, 1, 2, 3)[0])
    for s in range(2):
        @pl.when(sides[s][0])
        def _():
            lh_in[s].wait_recv()
            ih_in[s].wait_recv()
            inc = ih_recv[s].astype(F32)
            for t in range(F):
                spread(x2, s * (R + 1), t, lh_recv[s, t * W:(t + 1) * W].astype(F32)
                       + rot(*table(F + t), inc))

        @pl.when(jnp.logical_not(sides[s][0]))
        def _():
            x2[s * (R + 1)] = jnp.zeros((FW, K3), BF16)
    finish(0, acc[0] + taps(x2, wout, 0, 1, 0, 1)[0])
    finish(R - 1, acc[R - 1] + taps(x2, wout, R - 1, 1, 2, 3)[0])

    @pl.when(ih_out)
    def _():
        for j in range(2):
            ih[j].wait_send()

    for g in range(2):
        swap(g, True).wait_send()
    for k in range(steps):
        for g in range(2):
            hop(k, g).wait_send()
    for s in range(2):
        @pl.when(sides[s][0])
        def _():
            fh[s].wait_send()
            lh[s].wait_send()


def solution(mesh):
    n_tm, n_row = mesh.shape["tm"], mesh.shape["row"]
    steps = n_tm.bit_length() - 1
    assert n_tm == 1 << steps

    def shards(frames_in, state_in, modulus, angle, w_in, w_out):
        F, R, W, C = frames_in.shape
        assert R == 4 and steps > 1
        n_table = -(-(2 * F + 2 * steps) // 8) * 8
        anywhere = pl.BlockSpec(memory_space=pl.ANY)
        vmem = pl.BlockSpec(memory_space=pltpu.VMEM)
        dma = pltpu.SemaphoreType.DMA
        FW = F * W
        return pl.pallas_call(
            functools.partial(kernel, n_tm, n_row, steps),
            out_shape=jax.ShapeDtypeStruct(frames_in.shape, BF16),
            in_specs=[anywhere, anywhere, vmem, vmem, anywhere, anywhere],
            out_specs=vmem,
            scratch_shapes=[
                pltpu.VMEM((F, R, W, C), BF16),
                pltpu.VMEM((R, W, C), F32),
                pltpu.VMEM((9 * C, C), BF16),
                pltpu.VMEM((9 * C, C), BF16),
                pltpu.VMEM((R + 2, FW, 3 * C), BF16),
                pltpu.VMEM((R + 2, FW, 3 * C), BF16),
                pltpu.VMEM((R, FW, C), F32),
                pltpu.VMEM((R, FW, C), F32),
                pltpu.VMEM((n_table, C // 2), F32),
                pltpu.VMEM((n_table, C // 2), F32),
                pltpu.VMEM((R, W, C), F32),
                pltpu.VMEM((R, W, C), F32),
                pltpu.VMEM((steps, R, W, C), BF16),
                pltpu.VMEM((steps, R, W, C), BF16),
                pltpu.VMEM((2, F, W, C), BF16),
                pltpu.VMEM((2, FW, C), BF16),
                pltpu.VMEM((2, FW, C), BF16),
                pltpu.VMEM((2, W, C), BF16),
                pltpu.VMEM((2, W, C), BF16),
                pltpu.VMEM((R, W, C), BF16),
                pltpu.VMEM((R, W, C), BF16),
                dma((4,)),
                dma((steps, 2)),
                dma((steps, 2)),
                dma((2,)),
                dma((2,)),
                dma((2,)),
                dma((2,)),
                dma((2,)),
                dma((2,)),
                dma((2,)),
                dma((2,)),
            ],
            compiler_params=pltpu.CompilerParams(
                collective_id=0, has_side_effects=True, vmem_limit_bytes=56 * 1024 * 1024
            ),
        )(
            frames_in, state_in, modulus, angle.reshape(1, -1),
            w_in.reshape(9 * C, C), w_out.reshape(9 * C, C),
        )

    return jax.shard_map(
        shards,
        mesh=mesh,
        in_specs=(P("tm", "row", None, None), P("row", None, None), P(), P(), P(), P()),
        out_specs=P("tm", "row", None, None),
        check_vma=False,
    )
```
